256 devices in a mesh: pop: 16 (over y_hi, z), tp: 16 (over x, y_lo, core).
Axes of the slice: x: 4, y: 4 (y_hi: 2, y_lo: 2; y = y_hi * 2 + y_lo), z: 8, core: 2. Of those that a mesh axis runs over, the one named last changes fastest.
Arguments:
- tokens: bfloat16 [4096, 5120], P('pop'), may hold values from -6 to 6
- gate_weight: bfloat16 [5120, 14336], P('pop', 'tp'), may hold values from -0.078125 to 0.078125
- up_weight: bfloat16 [5120, 14336], P('pop', 'tp'), may hold values from -0.078125 to 0.078125
- down_weight: bfloat16 [5120, 14336], P('pop', 'tp'), may hold values from -0.0625 to 0.0625
- switch_velocity: float32 [5120, 14336], P('pop', 'tp'), may hold values from -6 to 6
- up_moment: float32 [5120, 14336], P('pop', 'tp'), may hold values from -6 to 6
- down_moment: float32 [5120, 14336], P('pop', 'tp'), may hold values from -6 to 6
- gate_in: bfloat16 [16, 5120], P('pop'), may hold values from -6 to 6
- switch_target_scaling: bfloat16 [16, 14336], P('pop', 'tp'), may hold values from -6 to 6
- up_in: bfloat16 [16, 5120], P('pop'), may hold values from -6 to 6
- up_output_factor: bfloat16 [16, 14336], P('pop', 'tp'), may hold values from -6 to 6
- down_in: bfloat16 [16, 14336], P('pop', 'tp'), may hold values from -6 to 6
- down_out: bfloat16 [16, 5120], P('pop'), may hold values from -6 to 6
- ranks: int32 [16], replicated, may hold values from 0 to 15, each once
- slot_member: int32 [16], replicated, may hold values from 0 to 15, each once
Outputs:
- evaluation: bfloat16 [16, 256, 5120], P('pop', None, 'tp')
- new_gate_moment: float32 [5120, 14336], P('pop', 'tp')
- new_up_moment: float32 [5120, 14336], P('pop', 'tp')
- new_down_moment: float32 [5120, 14336], P('pop', 'tp')
The draws below stay inside these ranges and needn't reach their ends.
Inputs may be any that keep to these rules, and one draw needn't show every extreme that they name: `ranks`: each member has one rank, each of 0 to 15 once. `slot_member`: each member is evaluated in exactly one slot.
All inputs are finite; a program needn't handle non-finite values.
Results may differ from the reference program's by a relative error of at most 0.028.
Values may be sent and summed in bfloat16 or wider, within the bound.
No kernel may reach another device: no remote copies, remote signals or barrier semaphores. Data moves between devices by JAX's collectives and lax.ppermute only.
A program may use at most 128 MiB of HBM per device.

```python
import math
import jax
import jax.numpy as jnp
from jax import lax

D = 5120
FF = 14336
ROWS = 256
MEMBERS_PER_SLICE = 1
M = 16
N_POP = 16
N_TP = 16


def with_spikes(entries, stream_key, source, target, parts, factor):
    owner, partner = [(jnp.arange(entries.shape[dim]) // (entries.shape[dim] // parts)).reshape([-1 if axis == dim else 1 for axis in range(entries.ndim)]) for dim in (source, target)]
    chosen = jax.random.permutation(stream_key, parts)[partner]
    strong = (owner == chosen) | (owner == (partner + parts // 2) % parts)
    return jnp.where(strong, factor * entries, entries)


def level_of(stream_key, shape, cuts, low, top_value):
    def one(dim, shards_of):
        heights = jax.random.uniform(jax.random.fold_in(jax.random.fold_in(stream_key, 6), dim), (shards_of,), jnp.float32, low / len(cuts), top_value / len(cuts))
        return jnp.repeat(jnp.exp(heights), shape[dim] // shards_of).reshape((-1,) + (1,) * (len(shape) - dim - 1))

    factor_of = one(*cuts[0])
    for cut in cuts[1:]:
        factor_of = factor_of * one(*cut)
    return factor_of


def bell_draw(key, dims, spread, most, pieces=(), kind=jnp.bfloat16):
    values = jax.random.normal(key, dims, jnp.float32) * spread
    if len(pieces) > 0:
        values = level_of(key, dims, pieces, -0.22, 0.18) * values
    return jnp.clip(values, min=-most, max=most).astype(kind)


def heavy_noise(rng, extent, width, most, cuts, heavy, held_as=jnp.bfloat16):
    drawn = width * jax.random.normal(rng, extent, jnp.float32)
    if cuts:
        drawn = drawn * level_of(rng, extent, cuts, -0.22, 0.18)
    return jnp.clip(with_spikes(drawn, jax.random.fold_in(rng, 3), *heavy), -most, most).astype(held_as)


def setup_inputs(seed: int = 0) -> dict:
    seeds = jax.random.split(jax.random.key(seed), 16)
    return {
        "tokens": bell_draw(seeds[0], (N_POP * ROWS, D), 1.0, 6.0, ((0, 16),)),
        "gate_weight": bell_draw(seeds[1], (D, FF), D ** -0.5, 0.078125, ((0, 16), (1, 16))),
        "up_weight": bell_draw(seeds[2], (D, FF), D ** -0.5, 0.078125, ((0, 16), (1, 16))),
        "down_weight": heavy_noise(seeds[3], (D, FF), FF ** -0.5, 0.0625, ((0, 16), (1, 16)), (1, 0, 16, 2.0)),
        "switch_velocity": bell_draw(seeds[4], (D, FF), 1.0, 6.0, ((0, 16), (1, 16)), jnp.float32),
        "up_moment": bell_draw(seeds[5], (D, FF), 1.0, 6.0, ((0, 16), (1, 16)), jnp.float32),
        "down_moment": bell_draw(seeds[6], (D, FF), 1.0, 6.0, ((0, 16), (1, 16)), jnp.float32),
        "gate_in": bell_draw(seeds[7], (M, D), 1.0, 6.0, ((0, 16),)),
        "switch_target_scaling": bell_draw(seeds[8], (M, FF), 1.0, 6.0, ((0, 16), (1, 16))),
        "up_in": bell_draw(seeds[9], (M, D), 1.0, 6.0, ((0, 16),)),
        "up_output_factor": bell_draw(seeds[10], (M, FF), 1.0, 6.0, ((0, 16), (1, 16))),
        "down_in": bell_draw(seeds[11], (M, FF), 1.0, 6.0, ((0, 16), (1, 16))),
        "down_out": bell_draw(seeds[12], (M, D), 1.0, 6.0, ((0, 16),)),
        "ranks": jax.random.permutation(seeds[13], M).astype(jnp.int32),
        "slot_member": jax.random.permutation(seeds[14], M).astype(jnp.int32),
    }


SIGMA = 0.005
BETA = 0.9

def member_output(inputs, base_gate, base_up, member, gate_in, switch_target_scaling, up_in, up_output_factor, down_in, down_out, down_weight):
    shift_gate = jnp.dot(inputs, gate_in[member], preferred_element_type=jnp.float32)
    shift_up = jnp.dot(inputs, up_in[member], preferred_element_type=jnp.float32)
    gate = base_gate + SIGMA * shift_gate[:, None] * switch_target_scaling[member].astype(jnp.float32)[None, :]
    upper = base_up + SIGMA * shift_up[:, None] * up_output_factor[member].astype(jnp.float32)[None, :]
    latent_neurons = (jax.nn.silu(gate) * upper).astype(jnp.bfloat16)
    block = FF // N_TP
    tail = down_out[member].astype(jnp.float32)
    entry = down_in[member]

    def shard_term(total, shard):
        start = (shard * block).astype(jnp.int32)
        piece_hidden = lax.dynamic_slice_in_dim(latent_neurons, start, block, 1)
        piece_weight = lax.dynamic_slice_in_dim(down_weight, start, block, 1)
        piece_entry = lax.dynamic_slice_in_dim(entry, start, block, 0)
        term = lax.dot_general(piece_hidden, piece_weight, (((1,), (1,)), ((), ())), preferred_element_type=jnp.float32)
        across_axis = jnp.dot(piece_hidden, piece_entry, preferred_element_type=jnp.float32)
        term = term + SIGMA * across_axis[:, None] * tail[None, :]
        rounded = lax.optimization_barrier(term.astype(jnp.bfloat16))
        return (total + rounded.astype(jnp.float32), None)
    total, _ = lax.scan(shard_term, jnp.zeros((ROWS, D), jnp.float32), jnp.arange(N_TP, dtype=jnp.int32))
    return total.astype(jnp.bfloat16)

def reference(tokens, gate_weight, up_weight, down_weight, switch_velocity, up_moment, down_moment, gate_in, switch_target_scaling, up_in, up_output_factor, down_in, down_out, ranks, slot_member):
    groups = tokens.reshape(N_POP, ROWS, D)
    members = slot_member.reshape(N_POP, MEMBERS_PER_SLICE)

    def group_eval(pair):
        inputs, ids = pair
        base_gate = jnp.dot(inputs, gate_weight, preferred_element_type=jnp.float32)
        base_up = jnp.dot(inputs, up_weight, preferred_element_type=jnp.float32)
        return lax.map(lambda member: member_output(inputs, base_gate, base_up, member, gate_in, switch_target_scaling, up_in, up_output_factor, down_in, down_out, down_weight), ids)
    evaluation = lax.map(group_eval, (groups, members)).reshape(M, ROWS, D)
    coef = (ranks.astype(jnp.float32) / (M - 1) - 0.5) / math.sqrt(M)

    def moment(old, left, right):
        weighted = coef[:, None] * left.astype(jnp.float32)
        return BETA * old + jnp.dot(weighted.T, right.astype(jnp.float32), precision=lax.Precision.HIGHEST)
    refreshed_gate = moment(switch_velocity, gate_in, switch_target_scaling)
    revised_raising = moment(up_moment, up_in, up_output_factor)
    new_down = moment(down_moment, down_out, down_in)
    return (evaluation, refreshed_gate, revised_raising, new_down)
```

```python
import math

import jax
import jax.numpy as jnp
from jax import lax
from jax.sharding import Mesh
from jax.sharding import PartitionSpec as P

SIGMA = 0.005
BETA = 0.9
F32 = jnp.float32
BF16 = jnp.bfloat16
NZ = 8
NX = 4


def dot(a, b):
    return jnp.dot(a, b, preferred_element_type=F32)


def at(array, index):
    return lax.dynamic_index_in_dim(array, index, 0, keepdims=False)


UP = [(i, (i + 1) % NZ) for i in range(NZ)]
DOWN = [(i, (i - 1) % NZ) for i in range(NZ)]
SWAP = [(0, 1), (1, 0)]


def ring(block):
    half = block.shape[0] // 2
    got = [block] + [None] * (NZ - 1)
    fore = back = block
    for k in range(1, NZ // 2):
        fore = lax.ppermute(fore, "z", UP)
        back = lax.ppermute(back, "z", DOWN)
        got[k], got[NZ - k] = fore, back
    got[NZ // 2] = jnp.concatenate(
        [lax.ppermute(fore[:half], "z", UP), lax.ppermute(back[half:], "z", DOWN)], axis=0
    )
    return got


def body(
    tokens,
    gate_weight,
    up_weight,
    down_weight,
    switch_velocity,
    up_moment,
    down_moment,
    gate_in,
    switch_target_scaling,
    up_in,
    up_output_factor,
    down_in,
    down_out,
    ranks,
    slot_member,
):
    rows, width = tokens.shape
    span, cols = gate_weight.shape
    members = ranks.shape[0]
    yh, z, x, yl, c = (lax.axis_index(name) for name in ("yh", "z", "x", "yl", "c"))
    position = yh * NZ + z
    half = width // 2

    factors = jnp.concatenate(
        [gate_in, up_in, down_out, switch_target_scaling, up_output_factor, down_in], axis=1
    )
    factors = lax.all_gather(factors, ("yh", "z"), axis=0, tiled=True)
    cuts = [width, 2 * width, 3 * width, 3 * width + cols, 3 * width + 2 * cols]
    full_gate_in, full_up_in, full_down_out, full_gate_out, full_up_out, full_down_in = jnp.split(
        factors, cuts, axis=1
    )

    mine = lax.dynamic_slice_in_dim(tokens, yh * half, half, 1)
    other = lax.dynamic_slice_in_dim(tokens, (1 - yh) * half, half, 1)
    both = jnp.concatenate([mine, lax.ppermute(other, "yh", SWAP)], axis=0)
    blocks = both.reshape(2 * rows, NZ, span).transpose(1, 0, 2)
    ordered = [at(blocks, (z - k) % NZ) for k in range(NZ)]

    def base(weight):
        total = None
        for piece, block in zip(ordered, ring(weight)):
            term = dot(piece, block)
            total = term if total is None else total + term
        sent = lax.ppermute(total[rows:].astype(BF16), "yh", SWAP)
        return total[:rows] + sent.astype(F32)

    base_gate = base(gate_weight)
    base_up = base(up_weight)

    own = at(slot_member, position)
    partner = at(slot_member, (1 - yh) * NZ + z)
    shift_gate = dot(tokens, at(full_gate_in, own))
    shift_up = dot(tokens, at(full_up_in, own))
    gate = base_gate + SIGMA * shift_gate[:, None] * at(full_gate_out, own).astype(F32)[None, :]
    upper = base_up + SIGMA * shift_up[:, None] * at(full_up_out, own).astype(F32)[None, :]
    hidden = (jax.nn.silu(gate) * upper).astype(BF16)
    theirs = lax.ppermute(hidden, "yh", SWAP)
    across = SIGMA * jnp.concatenate(
        [dot(hidden, at(full_down_in, own)), dot(theirs, at(full_down_in, partner))]
    )
    hiddens = jnp.concatenate([hidden, theirs], axis=0)
    tails = lax.dynamic_slice_in_dim(
        jnp.stack([at(full_down_out, own), at(full_down_out, partner)]), yh * half, half, 1
    ).astype(F32)
    tails = tails.reshape(2, NZ, span).transpose(1, 0, 2)

    parts = []
    for k, block in enumerate(ring(down_weight)):
        part = lax.dot_general(
            hiddens, block, (((1,), (1,)), ((), ())), preferred_element_type=F32
        )
        tail = jnp.repeat(at(tails, (z - k) % NZ), rows, axis=0)
        part = part + across[:, None] * tail
        parts.append(part.astype(BF16).reshape(2, rows, span))
    parts = jnp.stack(parts)

    keep = jnp.stack([at(parts, (z - (2 * j + c)) % NZ) for j in range(4)])
    send = jnp.stack([at(parts, (z - (2 * j + 1 - c)) % NZ) for j in range(4)])
    pairs = keep.astype(F32) + lax.ppermute(send, "c", SWAP).astype(F32)
    pairs = pairs.astype(BF16).reshape(2, 2, 2, rows, span).transpose(0, 2, 1, 3, 4)

    def piece_for(spot):
        group, high = spot // 2, spot % 2
        return at(at(pairs, high), group ^ yh)

    quad = piece_for(x).astype(F32)
    for d in range(1, NX):
        quad = quad + lax.ppermute(
            piece_for((x + d) % NX), "x", [(i, (i + d) % NX) for i in range(NX)]
        ).astype(F32)
    quad = quad.astype(BF16)

    def place(flip):
        perm = []
        for a in range(2):
            for b in range(NX):
                for e in range(2):
                    source = (a * NX + b) * 2 + e
                    target = ((b // 2) * NX + (a * 2 + b % 2)) * 2 + (e ^ flip)
                    perm.append((source, target))
        return lax.ppermute(at(quad, yl ^ flip), ("yh", "x", "yl"), perm).astype(F32)

    evaluation = (place(0) + place(1)).astype(BF16)[None]

    coef = (ranks.astype(F32) / (members - 1) - 0.5) / math.sqrt(members)

    def moment(old, left, right):
        left = lax.dynamic_slice_in_dim(left, position * span, span, 1)
        weighted = coef[:, None] * left.astype(F32)
        return BETA * old + jnp.dot(
            weighted.T, right.astype(F32), precision=lax.Precision.HIGHEST
        )

    new_gate = moment(switch_velocity, full_gate_in, full_gate_out)
    new_up = moment(up_moment, full_up_in, full_up_out)
    new_down = moment(down_moment, full_down_out, full_down_in)
    return (evaluation, new_gate, new_up, new_down)


def solution(mesh):
    fine = Mesh(mesh.devices.reshape(2, NZ, NX, 2, 2), ("yh", "z", "x", "yl", "c"))
    pop, tp = ("yh", "z"), ("x", "yl", "c")
    line, grid = P(pop, None), P(pop, tp)
    placed = (line,) + (grid,) * 6 + (line, grid, line, grid, grid, line, P(), P())
    return jax.shard_map(
        body,
        mesh=fine,
        in_specs=placed,
        out_specs=(P(pop, None, tp), grid, grid, grid),
        check_vma=False,
    )
```

```python
import math

import jax
import jax.numpy as jnp
from jax import lax
from jax.sharding import Mesh
from jax.sharding import PartitionSpec as P

SIGMA = 0.005
BETA = 0.9
F32 = jnp.float32
BF16 = jnp.bfloat16
NZ = 8
NX = 4


def dot(a, b):
    return jnp.dot(a, b, preferred_element_type=F32)


def at(array, index):
    starts = (index,) + (0,) * (array.ndim - 1)
    sizes = (1,) + array.shape[1:]
    return lax.dynamic_slice(array, starts, sizes, allow_negative_indices=False)[0]


UP = [(i, (i + 1) % NZ) for i in range(NZ)]
DOWN = [(i, (i - 1) % NZ) for i in range(NZ)]
SWAP = [(0, 1), (1, 0)]


def ring(block):
    half = block.shape[0] // 2
    got = [block] + [None] * (NZ - 1)
    fore = back = block
    for k in range(1, NZ // 2):
        fore = lax.ppermute(fore, "z", UP)
        back = lax.ppermute(back, "z", DOWN)
        got[k], got[NZ - k] = fore, back
    got[NZ // 2] = jnp.concatenate(
        [lax.ppermute(fore[:half], "z", UP), lax.ppermute(back[half:], "z", DOWN)], axis=0
    )
    return got


def body(
    tokens,
    gate_weight,
    up_weight,
    down_weight,
    switch_velocity,
    up_moment,
    down_moment,
    gate_in,
    switch_target_scaling,
    up_in,
    up_output_factor,
    down_in,
    down_out,
    ranks,
    slot_member,
):
    rows, width = tokens.shape
    span, cols = gate_weight.shape
    members = ranks.shape[0]
    yh, z, x, yl, c = (lax.axis_index(name) for name in ("yh", "z", "x", "yl", "c"))
    position = yh * NZ + z
    half = width // 2

    factors = jnp.concatenate(
        [gate_in, up_in, down_out, switch_target_scaling, up_output_factor, down_in], axis=1
    ).reshape(1, -1, 128)
    for step in (1, 2, 4):
        swap = [(i, i ^ step) for i in range(NZ)]
        factors = jnp.concatenate([factors, lax.ppermute(factors, "z", swap)], axis=0)
    factors = jnp.concatenate([factors, lax.ppermute(factors, "yh", SWAP)], axis=0)
    factors = factors.reshape(members, -1)
    cuts = [width, 2 * width, 3 * width, 3 * width + cols, 3 * width + 2 * cols]
    full_gate_in, full_up_in, full_down_out, full_gate_out, full_up_out, full_down_in = jnp.split(
        factors, cuts, axis=1
    )

    mine = lax.dynamic_slice_in_dim(tokens, yh * half, half, 1)
    other = lax.dynamic_slice_in_dim(tokens, (1 - yh) * half, half, 1)
    both = jnp.concatenate([mine, lax.ppermute(other, "yh", SWAP)], axis=0)
    blocks = both.reshape(2 * rows, NZ, span).transpose(1, 0, 2)
    ordered = [at(blocks, (z - k) & (NZ - 1)) for k in range(NZ)]

    def base(weight):
        total = None
        for piece, block in zip(ordered, ring(weight)):
            term = dot(piece, block)
            total = term if total is None else total + term
        sent = lax.ppermute(total[rows:].astype(BF16), "yh", SWAP)
        return total[:rows] + sent.astype(F32)

    base_gate = base(gate_weight)
    base_up = base(up_weight)

    own = at(slot_member, position) ^ position
    partner = at(slot_member, (1 - yh) * NZ + z) ^ position
    shift_gate = dot(tokens, at(full_gate_in, own))
    shift_up = dot(tokens, at(full_up_in, own))
    gate = base_gate + SIGMA * shift_gate[:, None] * at(full_gate_out, own).astype(F32)[None, :]
    upper = base_up + SIGMA * shift_up[:, None] * at(full_up_out, own).astype(F32)[None, :]
    hidden = (jax.nn.silu(gate) * upper).astype(BF16)
    theirs = lax.ppermute(hidden, "yh", SWAP)
    across = SIGMA * jnp.concatenate(
        [dot(hidden, at(full_down_in, own)), dot(theirs, at(full_down_in, partner))]
    )
    hiddens = jnp.concatenate([hidden, theirs], axis=0)
    tails = lax.dynamic_slice_in_dim(
        jnp.stack([at(full_down_out, own), at(full_down_out, partner)]), yh * half, half, 1
    ).astype(F32)
    tails = tails.reshape(2, NZ, span).transpose(1, 0, 2)

    parts = []
    for k, block in enumerate(ring(down_weight)):
        part = lax.dot_general(
            hiddens, block, (((1,), (1,)), ((), ())), preferred_element_type=F32
        )
        tail = jnp.repeat(at(tails, (z - k) & (NZ - 1)), rows, axis=0)
        part = part + across[:, None] * tail
        parts.append(part.astype(BF16).reshape(2, rows, span))
    parts = jnp.stack(parts)

    keep = jnp.stack([at(parts, (z - (2 * j + c)) & (NZ - 1)) for j in range(4)])
    send = jnp.stack([at(parts, (z - (2 * j + 1 - c)) & (NZ - 1)) for j in range(4)])
    pairs = keep.astype(F32) + lax.ppermute(send, "c", SWAP).astype(F32)
    pairs = pairs.astype(BF16).reshape(2, 2, 2, rows, span).transpose(0, 2, 1, 3, 4)

    def piece_for(spot):
        group, high = spot >> 1, spot & 1
        return at(at(pairs, high), group ^ yh)

    quad = piece_for(x).astype(F32)
    for d in range(1, NX):
        quad = quad + lax.ppermute(
            piece_for((x + d) & (NX - 1)), "x", [(i, (i + d) % NX) for i in range(NX)]
        ).astype(F32)
    quad = quad.astype(BF16)

    def place(flip):
        perm = []
        for a in range(2):
            for b in range(NX):
                for e in range(2):
                    source = (a * NX + b) * 2 + e
                    target = ((b // 2) * NX + (a * 2 + b % 2)) * 2 + (e ^ flip)
                    perm.append((source, target))
        return lax.ppermute(at(quad, yl ^ flip), ("yh", "x", "yl"), perm).astype(F32)

    evaluation = (place(0) + place(1)).astype(BF16)[None]

    coef = (ranks.astype(F32) / (members - 1) - 0.5) / math.sqrt(members)
    coef = coef[jnp.arange(members) ^ position]

    def moment(old, left, right):
        left = lax.dynamic_slice_in_dim(left, position * span, span, 1)
        weighted = coef[:, None] * left.astype(F32)
        return BETA * old + jnp.dot(
            weighted.T, right.astype(F32), precision=lax.Precision.HIGHEST
        )

    new_gate = moment(switch_velocity, full_gate_in, full_gate_out)
    new_up = moment(up_moment, full_up_in, full_up_out)
    new_down = moment(down_moment, full_down_out, full_down_in)
    return (evaluation, new_gate, new_up, new_down)


def solution(mesh):
    fine = Mesh(mesh.devices.reshape(2, NZ, NX, 2, 2), ("yh", "z", "x", "yl", "c"))
    pop, tp = ("yh", "z"), ("x", "yl", "c")
    line, grid = P(pop, None), P(pop, tp)
    placed = (line,) + (grid,) * 6 + (line, grid, line, grid, grid, line, P(), P())
    return jax.shard_map(
        body,
        mesh=fine,
        in_specs=placed,
        out_specs=(P(pop, None, tp), grid, grid, grid),
        check_vma=False,
    )
```

```python
import math

import jax
import jax.numpy as jnp
from jax import lax
from jax.sharding import Mesh
from jax.sharding import PartitionSpec as P

SIGMA = 0.005
BETA = 0.9
F32 = jnp.float32
BF16 = jnp.bfloat16
NZ = 8
NX = 4
TILES = NZ - 1


def dot(a, b):
    return jnp.dot(a, b, preferred_element_type=F32)


def dot_t(a, b):
    return lax.dot_general(a, b, (((1,), (1,)), ((), ())), preferred_element_type=F32)


def at(array, index):
    starts = (index,) + (0,) * (array.ndim - 1)
    sizes = (1,) + array.shape[1:]
    return lax.dynamic_slice(array, starts, sizes, allow_negative_indices=False)[0]


def window(array, start, size, axis):
    starts = [0] * array.ndim
    starts[axis] = start
    sizes = list(array.shape)
    sizes[axis] = size
    return lax.dynamic_slice(array, starts, sizes, allow_negative_indices=False)


SWAP = [(0, 1), (1, 0)]


def ring(block, empty=None):
    half = block.shape[0] // 2

    def step(array, k, sign):
        pairs = []
        for i in range(NZ):
            origin = (i - sign * (k - 1)) % NZ
            if origin != empty:
                pairs.append((i, (i + sign) % NZ))
        return lax.ppermute(array, "z", pairs)

    got = [block] + [None] * (NZ - 1)
    fore = back = block
    for k in range(1, NZ // 2):
        fore = step(fore, k, 1)
        back = step(back, k, -1)
        got[k], got[NZ - k] = fore, back
    last = NZ // 2
    got[last] = jnp.concatenate([step(fore[:half], last, 1), step(back[half:], last, -1)], axis=0)
    return got


def gather4(block, axis):
    near = [(i, i ^ 1) for i in range(4)]
    far = [(i, i ^ 3) for i in range(4)]
    half = block.shape[0] // 2
    one = lax.ppermute(block, axis, near)
    three = lax.ppermute(block, axis, far)
    top = lax.ppermute(three[:half], axis, near)
    low = lax.ppermute(one[half:], axis, far)
    return [block, one, jnp.concatenate([top, low], axis=0), three]


def body(
    tokens,
    gate_weight,
    up_weight,
    down_weight,
    switch_velocity,
    up_moment,
    down_moment,
    gate_in,
    switch_target_scaling,
    up_in,
    up_output_factor,
    down_in,
    down_out,
    ranks,
    slot_member,
):
    rows, width = tokens.shape
    span, cols = gate_weight.shape
    members = ranks.shape[0]
    tile = cols // TILES
    quarter = width // NX
    part_rows = rows // 4
    yh, z, x, yl, c = (lax.axis_index(name) for name in ("yh", "z", "x", "yl", "c"))
    position = yh * NZ + z
    mask = NZ - 1

    down_blocks = gather4(down_weight, ("yh", "yl"))

    piece = window(window(tokens, (yl * 2 + c) * part_rows, part_rows, 0), x * quarter, quarter, 1)
    token_ring = jnp.stack(ring(piece))
    token_ring = [at(token_ring, (z - i) & mask) for i in range(NZ)]

    def tile_of(spot):
        start = jnp.minimum(spot, TILES - 1) * tile
        return jnp.concatenate(
            [window(gate_weight, start, tile, 1), window(up_weight, start, tile, 1)], axis=1
        )

    tiles = [tile_of(z)]
    for d in range(1, NZ):
        pairs = [(i, (i + d) % NZ) for i in range(NZ) if (i + d) % NZ != TILES]
        tiles.append(lax.ppermute(tile_of((z + d) & mask), "z", pairs))

    inner = jnp.concatenate([gate_in, up_in, down_out], axis=0)
    inner = window(inner, x * quarter, quarter, 1)
    outer = jnp.concatenate([switch_target_scaling, up_output_factor, down_in], axis=0)
    cut = inner.size // 128
    factors = jnp.concatenate([inner.reshape(-1, 128), outer.reshape(-1, 128)], axis=0)[None]
    for step in (1, 2, 4):
        swap = [(i, i ^ step) for i in range(NZ)]
        factors = jnp.concatenate([factors, lax.ppermute(factors, "z", swap)], axis=0)
    factors = jnp.concatenate([factors, lax.ppermute(factors, "yh", SWAP)], axis=0)
    inner = factors[:, :cut].reshape(members * 3, quarter)
    outer = factors[:, cut:].reshape(members * 3, cols)

    flat = jnp.stack(gather4(jnp.concatenate(token_ring + [inner], axis=0), "x"))
    count = NZ * part_rows

    def side(high):
        return jnp.concatenate([at(flat, (high * 2) ^ x), at(flat, (high * 2 + 1) ^ x)], axis=1)

    near, far = side(yh), side(1 - yh)
    near_rows, far_rows = near[:count], far[:count]
    near_factors, far_factors = near[count:], far[count:]

    stacked = jnp.stack(tiles)
    own = jnp.concatenate([at(stacked, (z - i) & mask) for i in range(NZ)], axis=0)
    blocks = gather4(own, ("yh", "yl"))
    swapped = [lax.ppermute(block, "c", SWAP) for block in blocks]

    pair = jnp.stack([outer, lax.ppermute(outer, "yl", SWAP)])
    quad = jnp.stack([pair, lax.ppermute(pair, "c", SWAP)], axis=1)
    quad = quad.reshape(4, members, 3, cols)

    groups = yh * NZ + jnp.arange(NZ, dtype=jnp.int32)
    chosen = slot_member[groups] ^ position
    pick = jnp.repeat(
        (chosen[:, None] == jnp.arange(members, dtype=jnp.int32)[None, :]), part_rows, axis=0
    )
    pick_f32 = pick.astype(F32)
    pick = pick.astype(BF16)

    shifts = dot_t(near_rows, near_factors) + dot_t(far_rows, far_factors)
    shifts = shifts.reshape(count, members, 3)
    shift_gate = SIGMA * jnp.sum(shifts[:, :, 0] * pick_f32, axis=1)
    shift_up = SIGMA * jnp.sum(shifts[:, :, 1] * pick_f32, axis=1)

    start = jnp.minimum(z, TILES - 1) * tile
    here = window(quad, start, tile, 3)

    def hidden_of(fl):
        found = []
        for fc, source in enumerate((blocks, swapped)):
            both = dot(near_rows, source[fl]) + dot(far_rows, source[fl ^ 2])
            entry = here[2 * fl + fc]
            gate = both[:, :tile] + shift_gate[:, None] * dot(pick, entry[:, 0])
            upper = both[:, tile:] + shift_up[:, None] * dot(pick, entry[:, 1])
            found.append((jax.nn.silu(gate) * upper).astype(BF16))
        value = jnp.concatenate(found, axis=1)
        return jnp.where(z == TILES, jnp.zeros_like(value), value)

    down_swapped = [lax.ppermute(block, "c", SWAP) for block in down_blocks]

    def down_tiles(fh, fl):
        found = []
        for fc, source in enumerate((down_blocks, down_swapped)):
            block = source[fl ^ (2 * fh)]
            if fh == 0:
                block = jnp.concatenate([block, quad[2 * fl + fc, :, 2]], axis=0)
            found.append(block)
        return jnp.stack(
            [
                jnp.concatenate([block[:, j * tile : (j + 1) * tile] for block in found], axis=1)
                for j in range(TILES)
            ]
        )

    total = [None, None]
    for fl in (1, 0):
        arrived = ring(hidden_of(fl), TILES)
        weights = [down_tiles(fh, fl) for fh in range(2)]
        for k in (0, 1, 7, 2, 6, 3, 5, 4):
            index = jnp.minimum((z - k) & mask, TILES - 1)
            for fh in range(2):
                term = dot_t(arrived[k], at(weights[fh], index))
                total[fh] = term if total[fh] is None else total[fh] + term

    across = SIGMA * jnp.sum(total[0][:, span:] * pick_f32, axis=1)
    parts = []
    for fh, source in enumerate((near_factors, far_factors)):
        tail = window(source, z * span, span, 1).reshape(members, 3, span)[:, 2]
        term = total[fh][:, :span] + across[:, None] * dot(pick, tail)
        parts.append(
            term.astype(BF16).reshape(NZ, 2, part_rows // 2, span).transpose(1, 0, 2, 3)
        )
    parts = jnp.stack(parts).reshape(4, NZ, part_rows // 2, span)

    def piece_for(spot):
        return at(parts, ((spot >> 1) ^ yh) * 2 + (spot & 1))

    summed = piece_for(x).astype(F32)
    for f in range(1, NX):
        summed = summed + lax.ppermute(
            piece_for(x ^ f), "x", [(i, i ^ f) for i in range(NX)]
        ).astype(F32)
    summed = summed.astype(BF16)

    share = yl * 4 + c * 2 + (x & 1)
    placed = []
    for s in range(NZ):
        pairs = []
        for sz in range(NZ):
            for sx in range(NX):
                for sl in range(2):
                    for sc in range(2):
                        r = sl * 4 + sc * 2 + (sx & 1)
                        source = ((sz * NX + sx) * 2 + sl) * 2 + sc
                        tx = (sx >> 1) * 2 + (sz >> 2)
                        target = (((r ^ s) * NX + tx) * 2 + ((sz >> 1) & 1)) * 2 + (sz & 1)
                        pairs.append((source, target))
        chunk = at(summed, share ^ s)
        placed.append(lax.ppermute(chunk, ("z", "x", "yl", "c"), pairs))
    placed = jnp.stack(placed)
    evaluation = jnp.concatenate([at(placed, r ^ z) for r in range(NZ)], axis=0)[None]

    coef = (ranks.astype(F32) / (members - 1) - 0.5) / math.sqrt(members)
    coef = coef[jnp.arange(members) ^ position]
    spans = window(near_factors, z * span, span, 1).reshape(members, 3, span)
    outer = outer.reshape(members, 3, cols)

    def moment(old, left, right):
        weighted = coef[:, None] * left.astype(F32)
        return BETA * old + jnp.dot(
            weighted.T, right.astype(F32), precision=lax.Precision.HIGHEST
        )

    new_gate = moment(switch_velocity, spans[:, 0], outer[:, 0])
    new_up = moment(up_moment, spans[:, 1], outer[:, 1])
    new_down = moment(down_moment, spans[:, 2], outer[:, 2])
    return (evaluation, new_gate, new_up, new_down)


def solution(mesh):
    fine = Mesh(mesh.devices.reshape(2, NZ, NX, 2, 2), ("yh", "z", "x", "yl", "c"))
    pop, tp = ("yh", "z"), ("x", "yl", "c")
    line, grid = P(pop, None), P(pop, tp)
    placed = (line,) + (grid,) * 6 + (line, grid, line, grid, grid, line, P(), P())
    return jax.shard_map(
        body,
        mesh=fine,
        in_specs=placed,
        out_specs=(P(pop, None, tp), grid, grid, grid),
        check_vma=False,
    )
```

```python
import math

import jax
import jax.numpy as jnp
from jax import lax
from jax.sharding import Mesh
from jax.sharding import PartitionSpec as P

SIGMA = 0.005
BETA = 0.9
F32 = jnp.float32
BF16 = jnp.bfloat16
NZ = 8
NX = 4


def dot(a, b):
    return jnp.dot(a, b, preferred_element_type=F32)


def at(array, index):
    starts = (index,) + (0,) * (array.ndim - 1)
    sizes = (1,) + array.shape[1:]
    return lax.dynamic_slice(array, starts, sizes, allow_negative_indices=False)[0]


UP = [(i, (i + 1) % NZ) for i in range(NZ)]
DOWN = [(i, (i - 1) % NZ) for i in range(NZ)]
SWAP = [(0, 1), (1, 0)]


def behind(array, *others):
    return lax.optimization_barrier((array, *others))[0]


def ring(block, after=None):
    if after is not None:
        block = behind(block, *after)
    half = block.shape[0] // 2
    got = [block] + [None] * (NZ - 1)
    fore = back = block
    for k in range(1, NZ // 2):
        fore = lax.ppermute(fore, "z", UP)
        back = lax.ppermute(back, "z", DOWN)
        got[k], got[NZ - k] = fore, back
    got[NZ // 2] = jnp.concatenate(
        [lax.ppermute(fore[:half], "z", UP), lax.ppermute(back[half:], "z", DOWN)], axis=0
    )
    return got


def body(
    tokens,
    gate_weight,
    up_weight,
    down_weight,
    switch_velocity,
    up_moment,
    down_moment,
    gate_in,
    switch_target_scaling,
    up_in,
    up_output_factor,
    down_in,
    down_out,
    ranks,
    slot_member,
):
    rows, width = tokens.shape
    span, cols = gate_weight.shape
    members = ranks.shape[0]
    yh, z, x, yl, c = (lax.axis_index(name) for name in ("yh", "z", "x", "yl", "c"))
    position = yh * NZ + z
    half = width // 2

    mine = lax.dynamic_slice_in_dim(tokens, yh * half, half, 1)
    other = lax.dynamic_slice_in_dim(tokens, (1 - yh) * half, half, 1)
    theirs = lax.ppermute(other, "yh", SWAP)
    both = jnp.concatenate([mine, theirs], axis=0)
    blocks = both.reshape(2 * rows, NZ, span).transpose(1, 0, 2)
    ordered = [at(blocks, (z - k) & (NZ - 1)) for k in range(NZ)]

    gates = ring(gate_weight)
    ups = ring(up_weight)
    low = span // 2
    tops = ring(down_weight[:low], (gates[3], gates[5]))
    bottoms = ring(down_weight[low:], (ups[3], ups[5]))

    factors = jnp.concatenate(
        [gate_in, up_in, down_out, switch_target_scaling, up_output_factor, down_in], axis=1
    ).reshape(1, -1, 128)
    factors = behind(factors, theirs)
    for step in (4, 2, 1):
        swap = [(i, i ^ step) for i in range(NZ)]
        factors = jnp.stack([factors, lax.ppermute(factors, "z", swap)], axis=1)
        factors = factors.reshape(-1, *factors.shape[2:])
    factors = jnp.concatenate([factors, lax.ppermute(factors, "yh", SWAP)], axis=0)
    factors = factors.reshape(members, -1)
    cuts = [width, 2 * width, 3 * width, 3 * width + cols, 3 * width + 2 * cols]
    full_gate_in, full_up_in, full_down_out, full_gate_out, full_up_out, full_down_in = jnp.split(
        factors, cuts, axis=1
    )

    def base(found):
        total = None
        for piece, block in zip(ordered, found):
            term = dot(piece, block)
            total = term if total is None else total + term
        sent = lax.ppermute(total[rows:].astype(BF16), "yh", SWAP)
        return total[:rows] + sent.astype(F32)

    base_gate = base(gates)
    base_up = base(ups)

    own = at(slot_member, position) ^ position
    partner = at(slot_member, (1 - yh) * NZ + z) ^ position
    shift_gate = dot(tokens, at(full_gate_in, own))
    shift_up = dot(tokens, at(full_up_in, own))
    gate = base_gate + SIGMA * shift_gate[:, None] * at(full_gate_out, own).astype(F32)[None, :]
    upper = base_up + SIGMA * shift_up[:, None] * at(full_up_out, own).astype(F32)[None, :]
    hidden = (jax.nn.silu(gate) * upper).astype(BF16)
    guests = lax.ppermute(hidden, "yh", SWAP)
    across = SIGMA * jnp.concatenate(
        [dot(hidden, at(full_down_in, own)), dot(guests, at(full_down_in, partner))]
    )
    hiddens = jnp.concatenate([hidden, guests], axis=0)
    tails = lax.dynamic_slice_in_dim(
        jnp.stack([at(full_down_out, own), at(full_down_out, partner)]), yh * half, half, 1
    ).astype(F32)
    tails = tails.reshape(2, NZ, span).transpose(1, 0, 2)

    def part(k):
        block = jnp.concatenate([tops[k], bottoms[k]], axis=0)
        term = lax.dot_general(
            hiddens, block, (((1,), (1,)), ((), ())), preferred_element_type=F32
        )
        tail = jnp.repeat(at(tails, (z - k) & (NZ - 1)), rows, axis=0)
        term = term + across[:, None] * tail
        return term.astype(BF16).reshape(2, 2, rows // 2, span)

    def summed(group):
        parts = jnp.stack([part(k) for j in group for k in (j, j + 4)])
        parts = parts.transpose(2, 0, 1, 3, 4)
        pairs = at(parts, c).astype(F32) + lax.ppermute(at(parts, 1 - c), "c", SWAP).astype(F32)
        pairs = pairs.astype(BF16).reshape(len(group), 4, rows // 2, span)

        def piece_for(spot):
            found = []
            for i, j in enumerate(group):
                which = (((z - j) >> 2) ^ spot) & 1
                found.append(at(pairs[i], which * 2 + ((spot >> 1) ^ yh)))
            return jnp.stack(found)

        quad = piece_for(x).astype(F32)
        for d in range(1, NX):
            quad = quad + lax.ppermute(
                piece_for((x + d) & (NX - 1)), "x", [(i, (i + d) % NX) for i in range(NX)]
            ).astype(F32)
        return quad.astype(BF16)

    first = summed((1, 2, 3))
    quad = jnp.concatenate([summed((0,)), first], axis=0)

    def place(fl, fc):
        perm = []
        for a in range(2):
            for b in range(NX):
                for e in range(2):
                    for g in range(2):
                        source = ((a * NX + b) * 2 + e) * 2 + g
                        target = ((b // 2) * NX + (a * 2 + b % 2)) * 2 + (e ^ fl)
                        perm.append((source, target * 2 + (g ^ fc)))
        block = at(quad, (z - ((yl ^ fl) * 2 + (c ^ fc))) & 3)
        return lax.ppermute(block, ("yh", "x", "yl", "c"), perm).astype(F32)

    halves = jnp.stack([place(0, 0) + place(1, 0), place(0, 1) + place(1, 1)]).astype(BF16)
    evaluation = jnp.concatenate([at(halves, c), at(halves, 1 - c)], axis=0)[None]

    coef = (ranks.astype(F32) / (members - 1) - 0.5) / math.sqrt(members)
    coef = coef[jnp.arange(members) ^ position]

    def moment(old, left, right):
        left = lax.dynamic_slice_in_dim(left, position * span, span, 1)
        weighted = coef[:, None] * left.astype(F32)
        return BETA * old + jnp.dot(
            weighted.T, right.astype(F32), precision=lax.Precision.HIGHEST
        )

    new_gate = moment(switch_velocity, full_gate_in, full_gate_out)
    new_up = moment(up_moment, full_up_in, full_up_out)
    new_down = moment(down_moment, full_down_out, full_down_in)
    return (evaluation, new_gate, new_up, new_down)


def solution(mesh):
    fine = Mesh(mesh.devices.reshape(2, NZ, NX, 2, 2), ("yh", "z", "x", "yl", "c"))
    pop, tp = ("yh", "z"), ("x", "yl", "c")
    line, grid = P(pop, None), P(pop, tp)
    placed = (line,) + (grid,) * 6 + (line, grid, line, grid, grid, line, P(), P())
    return jax.shard_map(
        body,
        mesh=fine,
        in_specs=placed,
        out_specs=(P(pop, None, tp), grid, grid, grid),
        check_vma=False,
    )
```

```python
import functools
import math

import jax
import jax.numpy as jnp
from jax import lax
from jax.experimental import pallas as pl
from jax.experimental.pallas import tpu as pltpu
from jax.sharding import Mesh
from jax.sharding import PartitionSpec as P

SIGMA = 0.005
BETA = 0.9
F32 = jnp.float32
BF16 = jnp.bfloat16
NZ = 8
NX = 4
SPARE = 48
LIMIT = 48 * 1024 * 1024

UP = [(i, (i + 1) % NZ) for i in range(NZ)]
DOWN = [(i, (i - 1) % NZ) for i in range(NZ)]
SWAP = [(0, 1), (1, 0)]


def at(array, index):
    starts = (index,) + (0,) * (array.ndim - 1)
    sizes = (1,) + array.shape[1:]
    return lax.dynamic_slice(array, starts, sizes, allow_negative_indices=False)[0]


def window(array, start, size, axis):
    starts = [0] * array.ndim
    starts[axis] = start
    sizes = list(array.shape)
    sizes[axis] = size
    return lax.dynamic_slice(array, starts, sizes, allow_negative_indices=False)


def behind(array, *others):
    return lax.optimization_barrier((array, *others))[0]


def ring(block, after=None):
    if after is not None:
        block = behind(block, *after)
    half = block.shape[0] // 2
    got = [block] + [None] * (NZ - 1)
    fore = back = block
    for k in range(1, NZ // 2):
        fore = lax.ppermute(fore, "z", UP)
        back = lax.ppermute(back, "z", DOWN)
        got[k], got[NZ - k] = fore, back
    got[NZ // 2] = (lax.ppermute(fore[:half], "z", UP), lax.ppermute(back[half:], "z", DOWN))
    return got


def base_kernel(count, depth, *refs):
    pieces, blocks = refs[:count], refs[count : 2 * count]
    out = refs[-1]
    total = refs[2 * count][...] if len(refs) > 2 * count + 1 else None
    for piece, block in zip(pieces, blocks):
        term = jnp.dot(piece[...], block[:depth, :], preferred_element_type=F32)
        total = term if total is None else total + term
    out[...] = total


def base_sum(pieces, blocks, total=None):
    rows, depth = pieces[0].shape
    cols = blocks[0].shape[1]
    count = len(pieces)
    step = rows // 2
    extra = [] if total is None else [total]
    wide = pl.BlockSpec((step, cols), lambda i: (i, 0))
    return pl.pallas_call(
        functools.partial(base_kernel, count, depth),
        grid=(2,),
        in_specs=[pl.BlockSpec((step, depth), lambda i: (i, 0))] * count
        + [pl.BlockSpec(block.shape, lambda i: (0, 0)) for block in blocks]
        + [wide] * len(extra),
        out_specs=wide,
        out_shape=jax.ShapeDtypeStruct((rows, cols), F32),
        compiler_params=pltpu.CompilerParams(vmem_limit_bytes=LIMIT),
        cost_estimate=pl.CostEstimate(
            flops=2 * rows * cols * depth * count,
            bytes_accessed=count * (rows + cols) * depth * 2 + 4 * rows * cols,
            transcendentals=0,
        ),
    )(*pieces, *blocks, *extra)


def part_kernel(count, hidden, across, tails, *refs):
    blocks, keep, send = refs[:-2], refs[-2], refs[-1]
    per = len(blocks) // count
    left = hidden[...]
    size = left.shape[0] // 4
    for i in range(count):
        low = 0
        for block in blocks[i * per : (i + 1) * per]:
            high = low + block.shape[0]
            term = lax.dot_general(
                block[...], left, (((1,), (1,)), ((), ())), preferred_element_type=F32
            )
            for part in range(4):
                lanes = slice(part * size, (part + 1) * size)
                tail = tails[i, low:high, part % 2 : part % 2 + 1]
                value = term[:, lanes] + tail * across[:, lanes]
                out = keep if part < 2 else send
                spot = slice((part % 2) * size, (part % 2 + 1) * size)
                out[i, low:high, spot] = value.astype(BF16)
            low = high


def part_products(hidden, across, tails, blocks):
    count = len(blocks)
    flat = [piece for group in blocks for piece in group]
    rows, cols = hidden.shape
    span = tails.shape[1]
    shape = jax.ShapeDtypeStruct((count, span, rows // 2), BF16)
    return pl.pallas_call(
        functools.partial(part_kernel, count),
        out_shape=(shape, shape),
        compiler_params=pltpu.CompilerParams(vmem_limit_bytes=LIMIT),
        cost_estimate=pl.CostEstimate(
            flops=2 * rows * cols * span * count,
            bytes_accessed=2 * (rows * cols + count * span * (cols + rows)),
            transcendentals=0,
        ),
    )(hidden, across, tails, *flat)


def body(
    tokens,
    gate_weight,
    up_weight,
    down_weight,
    switch_velocity,
    up_moment,
    down_moment,
    gate_in,
    switch_target_scaling,
    up_in,
    up_output_factor,
    down_in,
    down_out,
    ranks,
    slot_member,
):
    rows, width = tokens.shape
    span, cols = gate_weight.shape
    members = ranks.shape[0]
    yh, z, x, yl, c = (lax.axis_index(name) for name in ("yh", "z", "x", "yl", "c"))
    position = yh * NZ + z
    mask = NZ - 1
    half = width // 2

    outer = jnp.concatenate([switch_target_scaling, up_output_factor, down_in], axis=0)
    inner = jnp.concatenate([gate_in, up_in, down_out], axis=1).reshape(-1, 128)
    fill = -inner.shape[0] % (cols // 128)
    inner = jnp.concatenate([inner, jnp.zeros((fill, 128), BF16)], axis=0).reshape(-1, cols)
    mine = jnp.concatenate([outer, inner], axis=0)
    pack = mine.shape[0]
    both = jnp.concatenate([mine, lax.ppermute(mine, "yh", SWAP)], axis=0)
    spare = jnp.zeros((SPARE - 2 * pack, cols), BF16)
    up_block = jnp.concatenate([up_weight, both, spare], axis=0)

    gates = ring(gate_weight)
    ups = ring(up_block)
    low = span // 2
    tops = ring(down_weight[:low], gates[4])
    bottoms = ring(down_weight[low:], ups[4])

    near = window(tokens, yh * half, half, 1)
    other = behind(window(tokens, (1 - yh) * half, half, 1), both)
    pair = jnp.concatenate([near, lax.ppermute(other, "yh", SWAP)], axis=0)
    blocks = pair.reshape(2 * rows, NZ, span).transpose(1, 0, 2)
    ordered = [at(blocks, (z - k) & mask) for k in range(NZ)]

    def base(found, fresh):
        early = (0, 1, 7, 2, 6)
        total = base_sum(
            [behind(ordered[k], found[3], found[5]) if k == 0 else ordered[k] for k in early],
            [found[k] for k in early],
        )
        last = jnp.concatenate(found[4], axis=0)
        total = base_sum(
            [ordered[k] for k in (3, 5, 4)], [found[3], found[5], last], total
        )
        sent = lax.ppermute(total[rows:].astype(BF16), "yh", SWAP)
        return total[:rows] + sent.astype(F32)

    base_gate = base(gates, gate_weight)
    base_up = base(ups, up_weight)

    ups[4] = jnp.concatenate(ups[4], axis=0)
    found = jnp.stack([block[span : span + 2 * pack] for block in ups]).reshape(NZ, 2, pack, cols)
    outer = found[:, :, :3].reshape(members, 3, cols)
    inner = found[:, :, 3:].reshape(members, -1)[:, : 3 * width].reshape(members, 3, width)

    def entry_of(member):
        return (((z - member) & mask) << 1) | ((member >> 3) ^ yh)

    own = entry_of(at(slot_member, position))
    partner = entry_of(at(slot_member, (1 - yh) * NZ + z))
    own_inner, own_outer = at(inner, own), at(outer, own)

    def shift(index):
        return SIGMA * jnp.dot(tokens, own_inner[index], preferred_element_type=F32)

    gate = base_gate + shift(0)[:, None] * own_outer[0].astype(F32)[None, :]
    upper = base_up + shift(1)[:, None] * own_outer[1].astype(F32)[None, :]
    hidden = (jax.nn.silu(gate) * upper).astype(BF16)
    guests = lax.ppermute(hidden, "yh", SWAP)
    short = rows // 2
    hiddens = jnp.concatenate(
        [
            window(source, side * short, short, 0)
            for side in (c, 1 - c)
            for source in (hidden, guests)
        ],
        axis=0,
    )
    lowers = jnp.stack([own_outer[2], at(outer, partner)[2]])
    across = lax.dot_general(
        lowers, hiddens, (((1,), (1,)), ((), ())), preferred_element_type=F32
    ).reshape(2, 2, 2, short)
    across = SIGMA * jnp.stack([across[0, :, 0], across[1, :, 1]], axis=1).reshape(1, -1)
    tails = window(jnp.stack([own_inner[2], at(inner, partner)[2]]), yh * half, half, 1)
    tails = tails.astype(F32).reshape(2, NZ, span).transpose(1, 2, 0)

    keeps, sends = [None] * NZ, [None] * NZ
    groups = [((0, 1, 7, 2, 6), None), ((3, 5), (3, 5)), ((4,), None)]
    for group, wait in groups:
        tail = jnp.stack([at(tails, (z - k) & mask) for k in group])
        found = [(tops[k], bottoms[k]) for k in group]
        found = [(*a, *b) if k == 4 else (a, b) for k, (a, b) in zip(group, found)]
        keep, send = part_products(hiddens, across, tail, found)
        for i, k in enumerate(group):
            keeps[k], sends[k] = keep[i], send[i]

    def summed(group):
        keep = jnp.stack([keeps[k] for j in group for k in (j, j + 4)])
        send = jnp.stack([sends[k] for j in group for k in (j, j + 4)])
        pairs = keep.astype(F32) + lax.ppermute(send, "c", SWAP).astype(F32)
        pairs = pairs.astype(BF16)

        def piece_for(spot):
            found = []
            for i, j in enumerate(group):
                which = (((z - j) >> 2) ^ spot) & 1
                found.append(
                    window(at(pairs, 2 * i + which), ((spot >> 1) ^ yh) * short, short, 1)
                )
            return jnp.stack(found)

        quad = piece_for(x).astype(F32)
        for d in range(1, NX):
            quad = quad + lax.ppermute(
                piece_for((x + d) & (NX - 1)), "x", [(i, (i + d) % NX) for i in range(NX)]
            ).astype(F32)
        return quad.astype(BF16)

    first = summed((1, 2, 3))
    quad = jnp.concatenate([summed((0,)), first], axis=0)

    def place(fl, fc):
        perm = []
        for a in range(2):
            for b in range(NX):
                for e in range(2):
                    for g in range(2):
                        source = ((a * NX + b) * 2 + e) * 2 + g
                        target = ((b // 2) * NX + (a * 2 + b % 2)) * 2 + (e ^ fl)
                        perm.append((source, target * 2 + (g ^ fc)))
        block = at(quad, (z - ((yl ^ fl) * 2 + (c ^ fc))) & 3)
        return lax.ppermute(block, ("yh", "x", "yl", "c"), perm).astype(F32)

    halves = jnp.stack([place(0, 0) + place(1, 0), place(0, 1) + place(1, 1)])
    halves = halves.transpose(0, 2, 1).astype(BF16)
    evaluation = jnp.concatenate([at(halves, c), at(halves, 1 - c)], axis=0)[None]

    coef = (ranks.astype(F32) / (members - 1) - 0.5) / math.sqrt(members)
    entries = jnp.arange(members, dtype=jnp.int32)
    coef = coef[((yh ^ (entries & 1)) << 3) | ((z - (entries >> 1)) & mask)]
    spans = window(inner, position * span, span, 2)

    def moment(old, left, right):
        weighted = coef[:, None] * left.astype(F32)
        return BETA * old + jnp.dot(
            weighted.T, right.astype(F32), precision=lax.Precision.HIGHEST
        )

    new_gate = moment(switch_velocity, spans[:, 0], outer[:, 0])
    new_up = moment(up_moment, spans[:, 1], outer[:, 1])
    new_down = moment(down_moment, spans[:, 2], outer[:, 2])
    return (evaluation, new_gate, new_up, new_down)


def solution(mesh):
    fine = Mesh(mesh.devices.reshape(2, NZ, NX, 2, 2), ("yh", "z", "x", "yl", "c"))
    pop, tp = ("yh", "z"), ("x", "yl", "c")
    line, grid = P(pop, None), P(pop, tp)
    placed = (line,) + (grid,) * 6 + (line, grid, line, grid, grid, line, P(), P())
    return jax.shard_map(
        body,
        mesh=fine,
        in_specs=placed,
        out_specs=(P(pop, None, tp), grid, grid, grid),
        check_vma=False,
    )
```

```python
import functools
import math

import jax
import jax.numpy as jnp
from jax import lax
from jax.experimental import pallas as pl
from jax.experimental.pallas import tpu as pltpu
from jax.sharding import Mesh
from jax.sharding import PartitionSpec as P

SIGMA = 0.005
BETA = 0.9
F32 = jnp.float32
BF16 = jnp.bfloat16
NZ = 8
NX = 4
SPARE = 48
LIMIT = 62 * 1024 * 1024

UP = [(i, (i + 1) % NZ) for i in range(NZ)]
DOWN = [(i, (i - 1) % NZ) for i in range(NZ)]
SWAP = [(0, 1), (1, 0)]


def at(array, index):
    starts = (index,) + (0,) * (array.ndim - 1)
    sizes = (1,) + array.shape[1:]
    return lax.dynamic_slice(array, starts, sizes, allow_negative_indices=False)[0]


def window(array, start, size, axis):
    starts = [0] * array.ndim
    starts[axis] = start
    sizes = list(array.shape)
    sizes[axis] = size
    return lax.dynamic_slice(array, starts, sizes, allow_negative_indices=False)


def behind(array, *others):
    return lax.optimization_barrier((array, *others))[0]


def ring(block, after=None):
    if after is not None:
        block = behind(block, *after)
    half = block.shape[0] // 2
    got = [block] + [None] * (NZ - 1)
    fore = back = block
    for k in range(1, NZ // 2):
        fore = lax.ppermute(fore, "z", UP)
        back = lax.ppermute(back, "z", DOWN)
        got[k], got[NZ - k] = fore, back
    got[NZ // 2] = (lax.ppermute(fore[:half], "z", UP), lax.ppermute(back[half:], "z", DOWN))
    return got


def base_kernel(count, depth, where, *refs):
    pieces, blocks = refs[:count], refs[count : 2 * count]
    out = refs[-1]
    total = refs[2 * count][...] if len(refs) > 2 * count + 1 else None
    for piece, block in zip(pieces, blocks):
        term = jnp.dot(piece[0], block[:depth, :], preferred_element_type=F32)
        total = term if total is None else total + term
    out[...] = total


def base_sum(where, pieces, steps, blocks, total=None):
    _, rows, depth = pieces.shape
    cols = blocks[0].shape[1]
    count = len(steps)
    half = rows // 2
    extra = [] if total is None else [total]
    wide = pl.BlockSpec((half, cols), lambda i, s: (i, 0))

    def place(k):
        return pl.BlockSpec((1, half, depth), lambda i, s: ((s[0] - k) & (NZ - 1), i, 0))

    return pl.pallas_call(
        functools.partial(base_kernel, count, depth),
        grid_spec=pltpu.PrefetchScalarGridSpec(
            num_scalar_prefetch=1,
            grid=(2,),
            in_specs=[place(k) for k in steps]
            + [pl.BlockSpec(block.shape, lambda i, s: (0, 0)) for block in blocks]
            + [wide] * len(extra),
            out_specs=wide,
        ),
        out_shape=jax.ShapeDtypeStruct((rows, cols), F32),
        compiler_params=pltpu.CompilerParams(vmem_limit_bytes=LIMIT),
        cost_estimate=pl.CostEstimate(
            flops=2 * rows * cols * depth * count,
            bytes_accessed=count * (rows + cols) * depth * 2 + 4 * rows * cols,
            transcendentals=0,
        ),
    )(where, *[pieces] * count, *blocks, *extra)


def part_kernel(where, hidden, across, tails, block, out):
    term = lax.dot_general(
        block[...], hidden[...], (((1,), (1,)), ((), ())), preferred_element_type=F32
    )
    size = hidden.shape[0] // 2
    for r in range(2):
        lanes = slice(r * size, (r + 1) * size)
        value = term[:, lanes] + tails[0, :, r : r + 1] * across[:, lanes]
        out[0, 0, :, lanes] = value.astype(BF16)


def part_products(where, hidden, across, tails, weight, n1):
    rows, cols = hidden.shape
    span = tails.shape[1]

    def block_of(i):
        return (i >> 1) * 4 + n1 * 2 + (i & 1)

    return pl.pallas_call(
        part_kernel,
        grid_spec=pltpu.PrefetchScalarGridSpec(
            num_scalar_prefetch=1,
            grid=(4,),
            in_specs=[
                pl.BlockSpec((rows, cols), lambda i, s: (0, 0)),
                pl.BlockSpec((1, rows), lambda i, s: (0, 0)),
                pl.BlockSpec((1, span, 2), lambda i, s: (block_of(i), 0, 0)),
                pl.BlockSpec((span, cols), lambda i, s: (block_of(i), 0)),
            ],
            out_specs=pl.BlockSpec(
                (1, 1, span, rows), lambda i, s: ((i & 1) ^ s[1], i >> 1, 0, 0)
            ),
        ),
        out_shape=jax.ShapeDtypeStruct((2, 2, span, rows), BF16),
        compiler_params=pltpu.CompilerParams(vmem_limit_bytes=LIMIT),
        cost_estimate=pl.CostEstimate(
            flops=2 * rows * cols * span * 4,
            bytes_accessed=2 * (rows * cols + 4 * span * (cols + rows)),
            transcendentals=0,
        ),
    )(where, hidden, across, tails, weight)


def body(
    tokens,
    gate_weight,
    up_weight,
    down_weight,
    switch_velocity,
    up_moment,
    down_moment,
    gate_in,
    switch_target_scaling,
    up_in,
    up_output_factor,
    down_in,
    down_out,
    ranks,
    slot_member,
):
    rows, width = tokens.shape
    span, cols = gate_weight.shape
    members = ranks.shape[0]
    yh, z, x, yl, c = (lax.axis_index(name) for name in ("yh", "z", "x", "yl", "c"))
    position = yh * NZ + z
    mask = NZ - 1
    half = width // 2

    outer = jnp.concatenate([switch_target_scaling, up_output_factor, down_in], axis=0)
    inner = jnp.concatenate([gate_in, up_in, down_out], axis=1).reshape(-1, 128)
    fill = -inner.shape[0] % (cols // 128)
    inner = jnp.concatenate([inner, jnp.zeros((fill, 128), BF16)], axis=0).reshape(-1, cols)
    depth = inner.shape[0]
    spare = jnp.zeros((SPARE // 2 - depth - 3, cols), BF16)
    mine = jnp.concatenate([inner, outer, spare], axis=0)
    both = jnp.concatenate([mine, lax.ppermute(mine, "yh", SWAP)], axis=0)
    up_block = jnp.concatenate([up_weight, both], axis=0)

    gates = ring(gate_weight)
    ups = ring(up_block)
    downs = lax.all_gather(behind(down_weight, gates[2]), "z", axis=0, tiled=True)

    where = jnp.stack([z, c])
    near = window(tokens, yh * half, half, 1)
    other = behind(window(tokens, (1 - yh) * half, half, 1), both)
    pair = jnp.concatenate([near, lax.ppermute(other, "yh", SWAP)], axis=0)
    blocks = pair.reshape(2 * rows, NZ, span).transpose(1, 0, 2)

    def base(found):
        early = (0, 1, 7, 2, 6)
        total = base_sum(
            behind(where, found[3], found[5]), blocks, early, [found[k] for k in early]
        )
        last = jnp.concatenate(found[4], axis=0)
        total = base_sum(where, blocks, (3, 5, 4), [found[3], found[5], last], total)
        sent = lax.ppermute(total[rows:].astype(BF16), "yh", SWAP)
        return total[:rows] + sent.astype(F32)

    base_gate = base(gates)
    base_up = base(ups)

    ups[4] = jnp.concatenate(ups[4], axis=0)
    found = jnp.stack([block[span:] for block in ups]).reshape(members, SPARE // 2, cols)
    outer = found[:, depth : depth + 3]

    def entry_of(member):
        return (((z - member) & mask) << 1) | ((member >> 3) ^ yh)

    own = entry_of(at(slot_member, position))
    partner = entry_of(at(slot_member, (1 - yh) * NZ + z))

    inner = found[:, :depth].reshape(members, -1)[:, : 3 * width].reshape(members, 3, width)
    own_inner, own_outer = at(inner, own), at(outer, own)
    shifts = SIGMA * lax.dot_general(
        tokens, own_inner[:2], (((1,), (1,)), ((), ())), preferred_element_type=F32
    )
    gate = base_gate + shifts[:, 0:1] * own_outer[0].astype(F32)[None, :]
    upper = base_up + shifts[:, 1:2] * own_outer[1].astype(F32)[None, :]
    hidden = (jax.nn.silu(gate) * upper).astype(BF16)
    guests = lax.ppermute(hidden, "yh", SWAP)
    hiddens = jnp.concatenate([hidden, guests], axis=0)
    across = [
        jnp.dot(hidden, own_outer[2], preferred_element_type=F32),
        jnp.dot(guests, at(outer, partner)[2], preferred_element_type=F32),
    ]
    across = SIGMA * jnp.concatenate(across).reshape(1, -1)
    tails = window(jnp.stack([own_inner[2], at(inner, partner)[2]]), yh * half, half, 1)
    tails = tails.astype(F32).reshape(2, NZ, span).transpose(1, 2, 0)

    quad = []
    for n1 in range(2):
        parts = part_products(where, hiddens, across, tails, downs, n1)
        pairs = parts[0].astype(F32) + lax.ppermute(parts[1], "c", SWAP).astype(F32)
        pairs = pairs.astype(BF16)

        def piece_for(spot):
            return window(at(pairs, spot & 1), ((spot >> 1) ^ yh) * rows, rows, 1)

        value = piece_for(x).astype(F32)
        for d in range(1, NX):
            value = value + lax.ppermute(
                piece_for((x + d) & (NX - 1)), "x", [(i, (i + d) % NX) for i in range(NX)]
            ).astype(F32)
        quad.append(value.astype(BF16))
    quad = jnp.stack(quad)

    def place(flip):
        perm = []
        for a in range(2):
            for b in range(NX):
                for e in range(2):
                    source = (a * NX + b) * 2 + e
                    target = ((b // 2) * NX + (a * 2 + b % 2)) * 2 + (e ^ flip)
                    perm.append((source, target))
        return lax.ppermute(at(quad, yl ^ flip), ("yh", "x", "yl"), perm).astype(F32)

    evaluation = (place(0) + place(1)).astype(BF16).T[None]

    coef = (ranks.astype(F32) / (members - 1) - 0.5) / math.sqrt(members)
    entries = jnp.arange(members, dtype=jnp.int32)
    coef = coef[((yh ^ (entries & 1)) << 3) | ((z - (entries >> 1)) & mask)]
    spans = window(inner, position * span, span, 2)

    def moment(old, left, right):
        weighted = coef[:, None] * left.astype(F32)
        return BETA * old + jnp.dot(
            weighted.T, right.astype(F32), precision=lax.Precision.HIGHEST
        )

    new_gate = moment(switch_velocity, spans[:, 0], outer[:, 0])
    new_up = moment(up_moment, spans[:, 1], outer[:, 1])
    new_down = moment(down_moment, spans[:, 2], outer[:, 2])
    return (evaluation, new_gate, new_up, new_down)


def solution(mesh):
    fine = Mesh(mesh.devices.reshape(2, NZ, NX, 2, 2), ("yh", "z", "x", "yl", "c"))
    pop, tp = ("yh", "z"), ("x", "yl", "c")
    line, grid = P(pop, None), P(pop, tp)
    placed = (line,) + (grid,) * 6 + (line, grid, line, grid, grid, line, P(), P())
    return jax.shard_map(
        body,
        mesh=fine,
        in_specs=placed,
        out_specs=(P(pop, None, tp), grid, grid, grid),
        check_vma=False,
    )
```

```python
import functools
import math

import jax
import jax.numpy as jnp
from jax import lax
from jax.experimental import pallas as pl
from jax.experimental.pallas import tpu as pltpu
from jax.sharding import Mesh
from jax.sharding import PartitionSpec as P

SIGMA = 0.005
BETA = 0.9
F32 = jnp.float32
BF16 = jnp.bfloat16
NZ = 8
NX = 4
SPARE = 48
LIMIT = 62 * 1024 * 1024

UP = [(i, (i + 1) % NZ) for i in range(NZ)]
DOWN = [(i, (i - 1) % NZ) for i in range(NZ)]
SWAP = [(0, 1), (1, 0)]


def at(array, index):
    starts = (index,) + (0,) * (array.ndim - 1)
    sizes = (1,) + array.shape[1:]
    return lax.dynamic_slice(array, starts, sizes, allow_negative_indices=False)[0]


def window(array, start, size, axis):
    starts = [0] * array.ndim
    starts[axis] = start
    sizes = list(array.shape)
    sizes[axis] = size
    return lax.dynamic_slice(array, starts, sizes, allow_negative_indices=False)


def behind(array, *others):
    return lax.optimization_barrier((array, *others))[0]


def ring(block, after=None):
    if after is not None:
        block = behind(block, *after)
    half = block.shape[0] // 2
    got = [block] + [None] * (NZ - 1)
    fore = back = block
    for k in range(1, NZ // 2):
        fore = lax.ppermute(fore, "z", UP)
        back = lax.ppermute(back, "z", DOWN)
        got[k], got[NZ - k] = fore, back
    got[NZ // 2] = (lax.ppermute(fore[:half], "z", UP), lax.ppermute(back[half:], "z", DOWN))
    return got


def base_kernel(count, depth, where, *refs):
    pieces, blocks = refs[:count], refs[count : 2 * count]
    out = refs[-1]
    total = refs[2 * count][...] if len(refs) > 2 * count + 1 else None
    for piece, block in zip(pieces, blocks):
        term = jnp.dot(piece[0], block[:depth, :], preferred_element_type=F32)
        total = term if total is None else total + term
    out[...] = total


def base_sum(where, pieces, steps, blocks, total=None):
    _, rows, depth = pieces.shape
    cols = blocks[0].shape[1]
    count = len(steps)
    half = rows // 2
    extra = [] if total is None else [total]
    wide = pl.BlockSpec((half, cols), lambda i, s: (i, 0))

    def place(k):
        return pl.BlockSpec((1, half, depth), lambda i, s: ((s[0] - k) & (NZ - 1), i, 0))

    return pl.pallas_call(
        functools.partial(base_kernel, count, depth),
        grid_spec=pltpu.PrefetchScalarGridSpec(
            num_scalar_prefetch=1,
            grid=(2,),
            in_specs=[place(k) for k in steps]
            + [pl.BlockSpec(block.shape, lambda i, s: (0, 0)) for block in blocks]
            + [wide] * len(extra),
            out_specs=wide,
        ),
        out_shape=jax.ShapeDtypeStruct((rows, cols), F32),
        compiler_params=pltpu.CompilerParams(vmem_limit_bytes=LIMIT),
        cost_estimate=pl.CostEstimate(
            flops=2 * rows * cols * depth * count,
            bytes_accessed=count * (rows + cols) * depth * 2 + 4 * rows * cols,
            transcendentals=0,
        ),
    )(where, *[pieces] * count, *blocks, *extra)


def part_kernel(where, hidden, across, tails, block, out):
    term = lax.dot_general(
        block[...], hidden[...], (((1,), (1,)), ((), ())), preferred_element_type=F32
    )
    size = hidden.shape[0] // 2
    for r in range(2):
        lanes = slice(r * size, (r + 1) * size)
        value = term[:, lanes] + tails[0, :, r : r + 1] * across[:, lanes]
        out[0, 0, :, lanes] = value.astype(BF16)


def part_products(where, hidden, across, tails, weight, n1):
    rows, cols = hidden.shape
    span = tails.shape[1]

    def block_of(i):
        return (i >> 1) * 4 + n1 * 2 + (i & 1)

    return pl.pallas_call(
        part_kernel,
        grid_spec=pltpu.PrefetchScalarGridSpec(
            num_scalar_prefetch=1,
            grid=(4,),
            in_specs=[
                pl.BlockSpec((rows, cols), lambda i, s: (0, 0)),
                pl.BlockSpec((1, rows), lambda i, s: (0, 0)),
                pl.BlockSpec((1, span, 2), lambda i, s: (block_of(i), 0, 0)),
                pl.BlockSpec((span, cols), lambda i, s: (block_of(i), 0)),
            ],
            out_specs=pl.BlockSpec(
                (1, 1, span, rows), lambda i, s: ((i & 1) ^ s[1], i >> 1, 0, 0)
            ),
        ),
        out_shape=jax.ShapeDtypeStruct((2, 2, span, rows), BF16),
        compiler_params=pltpu.CompilerParams(vmem_limit_bytes=LIMIT),
        cost_estimate=pl.CostEstimate(
            flops=2 * rows * cols * span * 4,
            bytes_accessed=2 * (rows * cols + 4 * span * (cols + rows)),
            transcendentals=0,
        ),
    )(where, hidden, across, tails, weight)


def body(
    tokens,
    gate_weight,
    up_weight,
    down_weight,
    switch_velocity,
    up_moment,
    down_moment,
    gate_in,
    switch_target_scaling,
    up_in,
    up_output_factor,
    down_in,
    down_out,
    ranks,
    slot_member,
):
    rows, width = tokens.shape
    span, cols = gate_weight.shape
    members = ranks.shape[0]
    yh, z, x, yl, c = (lax.axis_index(name) for name in ("yh", "z", "x", "yl", "c"))
    position = yh * NZ + z
    mask = NZ - 1
    half = width // 2

    outer = jnp.concatenate([switch_target_scaling, up_output_factor, down_in], axis=0)
    inner = jnp.concatenate([gate_in, up_in, down_out], axis=1).reshape(-1, 128)
    fill = -inner.shape[0] % (cols // 128)
    inner = jnp.concatenate([inner, jnp.zeros((fill, 128), BF16)], axis=0).reshape(-1, cols)
    depth = inner.shape[0]
    spare = jnp.zeros((SPARE // 2 - depth - 3, cols), BF16)
    mine = jnp.concatenate([inner, outer, spare], axis=0)
    both = jnp.concatenate([mine, lax.ppermute(mine, "yh", SWAP)], axis=0)
    up_block = jnp.concatenate([up_weight, both], axis=0)

    gates = ring(gate_weight)
    ups = ring(up_block)
    downs = lax.all_gather(down_weight, "z", axis=0, tiled=True)

    where = jnp.stack([z, c])
    near = window(tokens, yh * half, half, 1)
    other = behind(window(tokens, (1 - yh) * half, half, 1), both)
    pair = jnp.concatenate([near, lax.ppermute(other, "yh", SWAP)], axis=0)
    blocks = pair.reshape(2 * rows, NZ, span).transpose(1, 0, 2)

    def base(found):
        early = (0, 1, 7, 2, 6)
        total = base_sum(
            behind(where, found[3], found[5]), blocks, early, [found[k] for k in early]
        )
        last = jnp.concatenate(found[4], axis=0)
        total = base_sum(where, blocks, (3, 5, 4), [found[3], found[5], last], total)
        sent = lax.ppermute(total[rows:].astype(BF16), "yh", SWAP)
        return total[:rows] + sent.astype(F32)

    base_gate = base(gates)
    base_up = base(ups)

    ups[4] = jnp.concatenate(ups[4], axis=0)
    found = jnp.stack([block[span:] for block in ups]).reshape(members, SPARE // 2, cols)
    outer = found[:, depth : depth + 3]

    def entry_of(member):
        return (((z - member) & mask) << 1) | ((member >> 3) ^ yh)

    own = entry_of(at(slot_member, position))
    partner = entry_of(at(slot_member, (1 - yh) * NZ + z))

    inner = found[:, :depth].reshape(members, -1)[:, : 3 * width].reshape(members, 3, width)
    own_inner, own_outer = at(inner, own), at(outer, own)
    shifts = SIGMA * lax.dot_general(
        tokens, own_inner[:2], (((1,), (1,)), ((), ())), preferred_element_type=F32
    )
    gate = base_gate + shifts[:, 0:1] * own_outer[0].astype(F32)[None, :]
    upper = base_up + shifts[:, 1:2] * own_outer[1].astype(F32)[None, :]
    hidden = (jax.nn.silu(gate) * upper).astype(BF16)
    guests = lax.ppermute(hidden, "yh", SWAP)
    hiddens = jnp.concatenate([hidden, guests], axis=0)
    across = [
        jnp.dot(hidden, own_outer[2], preferred_element_type=F32),
        jnp.dot(guests, at(outer, partner)[2], preferred_element_type=F32),
    ]
    across = SIGMA * jnp.concatenate(across).reshape(1, -1)
    tails = window(jnp.stack([own_inner[2], at(inner, partner)[2]]), yh * half, half, 1)
    tails = tails.astype(F32).reshape(2, NZ, span).transpose(1, 2, 0)

    quad = []
    for n1 in range(2):
        parts = part_products(where, hiddens, across, tails, downs, n1)
        pairs = parts[0].astype(F32) + lax.ppermute(parts[1], "c", SWAP).astype(F32)
        pairs = pairs.astype(BF16)

        def piece_for(spot):
            return window(at(pairs, spot & 1), ((spot >> 1) ^ yh) * rows, rows, 1)

        value = piece_for(x).astype(F32)
        for d in range(1, NX):
            value = value + lax.ppermute(
                piece_for((x + d) & (NX - 1)), "x", [(i, (i + d) % NX) for i in range(NX)]
            ).astype(F32)
        quad.append(value.astype(BF16))
    quad = jnp.stack(quad)

    def place(flip):
        perm = []
        for a in range(2):
            for b in range(NX):
                for e in range(2):
                    source = (a * NX + b) * 2 + e
                    target = ((b // 2) * NX + (a * 2 + b % 2)) * 2 + (e ^ flip)
                    perm.append((source, target))
        return lax.ppermute(at(quad, yl ^ flip), ("yh", "x", "yl"), perm).astype(F32)

    evaluation = (place(0) + place(1)).astype(BF16).T[None]

    coef = (ranks.astype(F32) / (members - 1) - 0.5) / math.sqrt(members)
    entries = jnp.arange(members, dtype=jnp.int32)
    coef = coef[((yh ^ (entries & 1)) << 3) | ((z - (entries >> 1)) & mask)]
    spans = window(inner, position * span, span, 2)

    def moment(old, left, right):
        weighted = coef[:, None] * left.astype(F32)
        return BETA * old + jnp.dot(
            weighted.T, right.astype(F32), precision=lax.Precision.HIGHEST
        )

    new_gate = moment(switch_velocity, spans[:, 0], outer[:, 0])
    new_up = moment(up_moment, spans[:, 1], outer[:, 1])
    new_down = moment(down_moment, spans[:, 2], outer[:, 2])
    return (evaluation, new_gate, new_up, new_down)


def solution(mesh):
    fine = Mesh(mesh.devices.reshape(2, NZ, NX, 2, 2), ("yh", "z", "x", "yl", "c"))
    pop, tp = ("yh", "z"), ("x", "yl", "c")
    line, grid = P(pop, None), P(pop, tp)
    placed = (line,) + (grid,) * 6 + (line, grid, line, grid, grid, line, P(), P())
    return jax.shard_map(
        body,
        mesh=fine,
        in_specs=placed,
        out_specs=(P(pop, None, tp), grid, grid, grid),
        check_vma=False,
    )
```

```python
import math

import jax
import jax.numpy as jnp
from jax import lax
from jax.sharding import Mesh
from jax.sharding import PartitionSpec as P

SIGMA = 0.005
BETA = 0.9
F32 = jnp.float32
BF16 = jnp.bfloat16
NZ = 8
NX = 4


def dot(a, b):
    return jnp.dot(a, b, preferred_element_type=F32)


def at(array, index):
    starts = (index,) + (0,) * (array.ndim - 1)
    sizes = (1,) + array.shape[1:]
    return lax.dynamic_slice(array, starts, sizes, allow_negative_indices=False)[0]


UP = [(i, (i + 1) % NZ) for i in range(NZ)]
DOWN = [(i, (i - 1) % NZ) for i in range(NZ)]
SWAP = [(0, 1), (1, 0)]


def behind(array, *others):
    return lax.optimization_barrier((array, *others))[0]


def ring(block):
    half = block.shape[0] // 2
    got = [block] + [None] * (NZ - 1)
    fore = back = block
    for k in range(1, NZ // 2):
        fore = lax.ppermute(fore, "z", UP)
        back = lax.ppermute(back, "z", DOWN)
        got[k], got[NZ - k] = fore, back
    got[NZ // 2] = jnp.concatenate(
        [lax.ppermute(fore[:half], "z", UP), lax.ppermute(back[half:], "z", DOWN)], axis=0
    )
    return got


def body(
    tokens,
    gate_weight,
    up_weight,
    down_weight,
    switch_velocity,
    up_moment,
    down_moment,
    gate_in,
    switch_target_scaling,
    up_in,
    up_output_factor,
    down_in,
    down_out,
    ranks,
    slot_member,
):
    rows, width = tokens.shape
    span, cols = gate_weight.shape
    members = ranks.shape[0]
    yh, z, x, yl, c = (lax.axis_index(name) for name in ("yh", "z", "x", "yl", "c"))
    position = yh * NZ + z
    half = width // 2

    gates, ups, downs = ring(gate_weight), ring(up_weight), ring(down_weight)

    factors = jnp.concatenate(
        [gate_in, up_in, down_out, switch_target_scaling, up_output_factor, down_in], axis=1
    ).reshape(1, -1, 128)
    turns = [[found[k] for found in (gates, ups) for k in (near, NZ - near)] for near in (1, 2)]
    turns += [[found[3], found[5]] for found in (gates, ups)]
    for step, turn in zip((1, 2, 4), turns):
        swap = [(i, i ^ step) for i in range(NZ)]
        factors = behind(factors, *turn)
        factors = jnp.concatenate([factors, lax.ppermute(factors, "z", swap)], axis=0)
    factors = behind(factors, *turns[3])
    factors = jnp.concatenate([factors, lax.ppermute(factors, "yh", SWAP)], axis=0)
    factors = factors.reshape(members, -1)
    cuts = [width, 2 * width, 3 * width, 3 * width + cols, 3 * width + 2 * cols]
    full_gate_in, full_up_in, full_down_out, full_gate_out, full_up_out, full_down_in = jnp.split(
        factors, cuts, axis=1
    )

    mine = lax.dynamic_slice_in_dim(tokens, yh * half, half, 1)
    other = lax.dynamic_slice_in_dim(tokens, (1 - yh) * half, half, 1)
    both = jnp.concatenate([mine, lax.ppermute(other, "yh", SWAP)], axis=0)
    blocks = both.reshape(2 * rows, NZ, span).transpose(1, 0, 2)
    ordered = [at(blocks, (z - k) & (NZ - 1)) for k in range(NZ)]

    def base(found):
        total = None
        for piece, block in zip(ordered, found):
            term = dot(piece, block)
            total = term if total is None else total + term
        sent = lax.ppermute(total[rows:].astype(BF16), "yh", SWAP)
        return total[:rows] + sent.astype(F32)

    base_gate = base(gates)
    base_up = base(ups)

    own = at(slot_member, position) ^ position
    partner = at(slot_member, (1 - yh) * NZ + z) ^ position
    shift_gate = dot(tokens, at(full_gate_in, own))
    shift_up = dot(tokens, at(full_up_in, own))
    gate = base_gate + SIGMA * shift_gate[:, None] * at(full_gate_out, own).astype(F32)[None, :]
    upper = base_up + SIGMA * shift_up[:, None] * at(full_up_out, own).astype(F32)[None, :]
    hidden = (jax.nn.silu(gate) * upper).astype(BF16)
    theirs = lax.ppermute(hidden, "yh", SWAP)
    across = SIGMA * jnp.concatenate(
        [dot(hidden, at(full_down_in, own)), dot(theirs, at(full_down_in, partner))]
    )
    hiddens = jnp.concatenate([hidden, theirs], axis=0)
    tails = lax.dynamic_slice_in_dim(
        jnp.stack([at(full_down_out, own), at(full_down_out, partner)]), yh * half, half, 1
    ).astype(F32)
    tails = tails.reshape(2, NZ, span).transpose(1, 0, 2)

    parts = []
    for k, block in enumerate(downs):
        part = lax.dot_general(
            hiddens, block, (((1,), (1,)), ((), ())), preferred_element_type=F32
        )
        tail = jnp.repeat(at(tails, (z - k) & (NZ - 1)), rows, axis=0)
        part = part + across[:, None] * tail
        parts.append(part.astype(BF16).reshape(2, rows, span))
    parts = jnp.stack(parts)

    keep = jnp.stack([at(parts, (z - (2 * j + c)) & (NZ - 1)) for j in range(4)])
    send = jnp.stack([at(parts, (z - (2 * j + 1 - c)) & (NZ - 1)) for j in range(4)])
    pairs = keep.astype(F32) + lax.ppermute(send, "c", SWAP).astype(F32)
    pairs = pairs.astype(BF16).reshape(2, 2, 2, rows, span).transpose(0, 2, 1, 3, 4)

    def piece_for(spot):
        group, high = spot >> 1, spot & 1
        return at(at(pairs, high), group ^ yh)

    quad = piece_for(x).astype(F32)
    for d in range(1, NX):
        quad = quad + lax.ppermute(
            piece_for((x + d) & (NX - 1)), "x", [(i, (i + d) % NX) for i in range(NX)]
        ).astype(F32)
    quad = quad.astype(BF16)

    def place(flip):
        perm = []
        for a in range(2):
            for b in range(NX):
                for e in range(2):
                    source = (a * NX + b) * 2 + e
                    target = ((b // 2) * NX + (a * 2 + b % 2)) * 2 + (e ^ flip)
                    perm.append((source, target))
        return lax.ppermute(at(quad, yl ^ flip), ("yh", "x", "yl"), perm).astype(F32)

    evaluation = (place(0) + place(1)).astype(BF16)[None]

    coef = (ranks.astype(F32) / (members - 1) - 0.5) / math.sqrt(members)
    coef = coef[jnp.arange(members) ^ position]

    def moment(old, left, right):
        left = lax.dynamic_slice_in_dim(left, position * span, span, 1)
        weighted = coef[:, None] * left.astype(F32)
        return BETA * old + jnp.dot(
            weighted.T, right.astype(F32), precision=lax.Precision.HIGHEST
        )

    new_gate = moment(switch_velocity, full_gate_in, full_gate_out)
    new_up = moment(up_moment, full_up_in, full_up_out)
    new_down = moment(down_moment, full_down_out, full_down_in)
    return (evaluation, new_gate, new_up, new_down)


def solution(mesh):
    fine = Mesh(mesh.devices.reshape(2, NZ, NX, 2, 2), ("yh", "z", "x", "yl", "c"))
    pop, tp = ("yh", "z"), ("x", "yl", "c")
    line, grid = P(pop, None), P(pop, tp)
    placed = (line,) + (grid,) * 6 + (line, grid, line, grid, grid, line, P(), P())
    return jax.shard_map(
        body,
        mesh=fine,
        in_specs=placed,
        out_specs=(P(pop, None, tp), grid, grid, grid),
        check_vma=False,
    )
```
